32 devices in a mesh: groups: 2 (over y), gx: 8 (over z, x), gy: 2 (over core).
Axes of the slice: x: 2, y: 2, z: 4, core: 2. Of those that a mesh axis runs over, the one named last changes fastest.
Arguments:
- tokens: bfloat16 [256, 18432], P(('groups', 'gx'), 'gy'), parts along dimension 0, may hold values from -6 to 6
- up_weight: bfloat16 [40960, 18432], P('gx', 'gy'), may hold values from -0.046875 to 0.046875
Outputs:
- projected: bfloat16 [256, 40960], P(('groups', 'gy'), 'gx'), parts along dimension 0
The draws below stay inside these ranges and needn't reach their ends.
There are 2 independent parts, one for each index of `groups`. The reference program is written for one: setup_inputs(seed, part) draws one part's arguments, and reference() takes and returns one part's arrays. A program takes and returns all parts, laid end to end along the dimension named above; an argument that names none is the same for every part. Nothing has to cross between parts.
All inputs are finite; a program needn't handle non-finite values.
Results may differ from the reference program's by a relative error of at most 0.001.
Values may be sent and summed in bfloat16 or wider, within the bound.
A program may use at most 192 MiB of HBM per device.

```python
import jax
import jax.numpy as jnp

D = 18432
F = 40960
TOKENS = 128


def block_levels(rng, shape, shards, smallest, high):
    def one(axis_at, shards_of):
        draws = jax.random.uniform(jax.random.fold_in(jax.random.fold_in(rng, 6), axis_at), (shards_of,), jnp.float32, smallest / len(shards), high / len(shards))
        return jnp.repeat(jnp.exp(draws), shape[axis_at] // shards_of).reshape((-1,) + (1,) * (len(shape) - axis_at - 1))

    factor_of = one(*shards[0])
    for cut in shards[1:]:
        factor_of = factor_of * one(*cut)
    return factor_of


def gaussian(own_key, extent, scale, bound, split=(), dtype=jnp.bfloat16):
    loudness = block_levels(own_key, extent, split, -0.22, 0.18) if split else 1.0
    drawn = jax.random.normal(own_key, extent, jnp.float32) * scale * loudness
    return jnp.minimum(jnp.maximum(drawn, -bound), bound).astype(dtype)


def setup_inputs(seed: int = 0, part: int = 0) -> dict:
    splits = jax.random.split(jax.random.key(seed), 3)
    own_keys = jax.random.split(jax.random.fold_in(splits[2], part), 3)
    return {
        "tokens": gaussian(own_keys[0], (TOKENS, D), 1.0, 6.0, ((0, 8), (1, 2))),
        "up_weight": gaussian(splits[1], (F, D), D ** -0.5, 0.046875, ((0, 8), (1, 2))),
    }


def reference(tokens, up_weight):
    summed = jnp.dot(tokens, up_weight.T, preferred_element_type=jnp.float32)
    return summed.astype(jnp.bfloat16)
```

```python
import functools

import jax
import jax.numpy as jnp
from jax import lax
from jax.experimental import pallas as pl
from jax.experimental.pallas import tpu as pltpu
from jax.sharding import PartitionSpec as P

MESH = pl.DeviceIdType.MESH
SLACK = 0


def ring_place(index, n):
    odd, half = lax.rem(index, 2), lax.div(index, 2)
    return odd * (n - 1 - half) + (1 - odd) * half


def ring_index(place, n):
    down = lax.div(place, n // 2)
    return (1 - down) * 2 * place + down * (2 * (n - 1 - place) + 1)


def kernel(
    n, pieces, halves, tiles, slots,
    tokens_ref, weight_ref, out_ref,
    gathered, weights, acc, parts, arrived, result,
    own_sem, weight_sem, send_sem, recv_sem, part_send, part_recv, out_sem,
):
    me, core = lax.axis_index("gx"), lax.axis_index("gy")
    rows, width = tokens_ref.shape[0], gathered.shape[2]
    block, tile = weights.shape[1], weights.shape[1] // tiles
    hops = n // 2
    place = ring_place(me, n)
    neighbours = tuple(ring_index(lax.rem(place + d, n), n) for d in (1, n - 1))
    blocks = pieces * halves

    def weight_copy(piece, half):
        slot = lax.rem(piece * halves + half, slots)
        return pltpu.make_async_copy(
            weight_ref.at[
                pl.ds(half * block, block), pl.ds(pl.multiple_of(piece * width, 128), width)
            ],
            weights.at[slot],
            weight_sem.at[slot],
        )

    def own_columns(piece):
        return tokens_ref.at[:, pl.ds(pl.multiple_of(piece * width, 128), width)]

    def rows_of(owner):
        return pl.ds(pl.multiple_of(owner * rows, rows), rows)

    def own_copy(piece):
        return pltpu.make_async_copy(
            own_columns(piece), gathered.at[piece, rows_of(me)], own_sem.at[piece]
        )

    def ring_copy(way, piece, hop):
        back = n - hop if way == 0 else hop
        held = gathered.at[piece, rows_of(ring_index(lax.rem(place + back, n), n))]
        return pltpu.make_async_remote_copy(
            src_ref=own_columns(piece) if hop == 0 else held,
            dst_ref=held,
            send_sem=send_sem.at[way, piece, hop],
            recv_sem=recv_sem.at[way, piece, hop],
            device_id={"gx": neighbours[way]},
            device_id_type=MESH,
        )

    def each_way(piece, hop, act):
        if hop < hops - 1:
            act(0)
            act(1)
        elif isinstance(piece, int):
            act(piece % 2)
        else:
            pl.when(lax.rem(piece, 2) == 0)(lambda: act(0))
            pl.when(lax.rem(piece, 2) == 1)(lambda: act(1))

    def stage(piece, hop):
        if hop >= 1:
            each_way(piece, hop - 1, lambda way: ring_copy(way, piece, hop - 1).wait_recv())
        if hop < hops:
            each_way(piece, hop, lambda way: ring_copy(way, piece, hop).start())

    def tick(step, extra):
        for hop in range(hops, -1, -1):
            if (extra - hop) % halves:
                continue
            piece = step + (extra - hop) // halves
            if isinstance(step, int):
                if 0 <= piece < pieces:
                    stage(piece, hop)
            else:
                pl.when(piece < pieces)(functools.partial(stage, piece, hop))

    for b in range(min(slots, blocks)):
        weight_copy(b // halves, b % halves).start()

    barrier = pltpu.get_barrier_semaphore()
    for neighbour in neighbours:
        pl.semaphore_signal(barrier, inc=1, device_id={"gx": neighbour}, device_id_type=MESH)
    pl.semaphore_signal(barrier, inc=1, device_id={"gy": 1 - core}, device_id_type=MESH)
    pl.semaphore_wait(barrier, 3)

    ahead = hops + SLACK
    tick(0, 0)
    for piece in range(pieces):
        own_copy(piece).start()
    for t in range(1, ahead):
        tick(t // halves, t % halves)
    acc[...] = jnp.zeros_like(acc)

    def product(piece, half, tile_at):
        slot = lax.rem(piece * halves + half, slots)
        at = pl.ds(tile_at[0], tile_at[1])
        return lax.dot_general(
            weights[slot, at, :], gathered[piece], (((1,), (1,)), ((), ())),
            preferred_element_type=jnp.float32,
        )

    @pl.loop(0, pieces - 1)
    def _(piece):
        for half in range(halves):
            tick(piece, half + ahead)
            if half == 0:
                own_copy(piece).wait()
            weight_copy(piece, half).wait()
            acc[pl.ds(half * block, block), :] += product(piece, half, (0, block))
            later = piece * halves + half + slots

            @pl.when(later < blocks)
            def _():
                weight_copy(lax.div(later, halves), lax.rem(later, halves)).start()

    last = pieces - 1
    for extra in range(halves):
        tick(last, extra + ahead)
    own_copy(last).wait()
    mine = parts.shape[1]

    def part_copy(j):
        at = pl.ds(j * tile, tile)
        return pltpu.make_async_remote_copy(
            src_ref=parts.at[1 - core, :, at],
            dst_ref=arrived.at[:, at],
            send_sem=part_send.at[j],
            recv_sem=part_recv.at[j],
            device_id={"gy": 1 - core},
            device_id_type=MESH,
        )

    def out_copy(j):
        at = pl.ds(j * tile, tile)
        return pltpu.make_async_copy(result.at[:, at], out_ref.at[:, at], out_sem.at[j])

    def combine(j):
        at = pl.ds(j * tile, tile)
        part_copy(j).wait_recv()
        result[:, at] = (parts[core, :, at] + arrived[:, at]).astype(result.dtype)
        out_copy(j).start()

    total = halves * tiles
    for j in range(total):
        half, within = j // tiles, j % tiles
        if within == 0:
            weight_copy(last, half).wait()
        summed = acc[pl.ds(j * tile, tile), :] + product(last, half, (within * tile, tile))
        turned = summed.T
        at = pl.ds(j * tile, tile)
        parts[0, :, at] = turned[:mine]
        parts[1, :, at] = turned[mine:]
        part_copy(j).start()
        if j >= 2:
            combine(j - 2)
    for j in range(max(total - 2, 0), total):
        combine(j)

    @pl.loop(0, pieces)
    def _(piece):
        for hop in range(hops):
            each_way(piece, hop, lambda way: ring_copy(way, piece, hop).wait_send())

    for j in range(total):
        part_copy(j).wait_send()
        out_copy(j).wait()


def on_device(n, tokens, up_weight):
    rows, depth = tokens.shape
    hidden = up_weight.shape[0]
    width = 1024 if depth % 1024 == 0 else 128
    pieces = depth // width
    halves = 2 if hidden % 256 == 0 else 1
    block = hidden // halves
    tiles = 2 if block % 256 == 0 else 1
    slots = min(8, pieces * halves)
    every, mine = rows * n, rows * n // 2
    dma = pltpu.SemaphoreType.DMA
    return pl.pallas_call(
        functools.partial(kernel, n, pieces, halves, tiles, slots),
        out_shape=jax.ShapeDtypeStruct((mine, hidden), jnp.bfloat16),
        in_specs=[pl.BlockSpec(memory_space=pl.ANY)] * 2,
        out_specs=pl.BlockSpec(memory_space=pl.ANY),
        scratch_shapes=[
            pltpu.VMEM((pieces, every, width), jnp.bfloat16),
            pltpu.VMEM((slots, block, width), jnp.bfloat16),
            pltpu.VMEM((hidden, every), jnp.float32),
            pltpu.VMEM((2, mine, hidden), jnp.float32),
            pltpu.VMEM((mine, hidden), jnp.float32),
            pltpu.VMEM((mine, hidden), jnp.bfloat16),
            dma((pieces,)),
            dma((slots,)),
            dma((2, pieces, n // 2)),
            dma((2, pieces, n // 2)),
            dma((halves * tiles,)),
            dma((halves * tiles,)),
            dma((halves * tiles,)),
        ],
        compiler_params=pltpu.CompilerParams(
            collective_id=0, has_side_effects=True, vmem_limit_bytes=58 * 2**20
        ),
        cost_estimate=pl.CostEstimate(
            flops=2 * every * hidden * depth, bytes_accessed=2 * hidden * depth, transcendentals=0
        ),
    )(tokens, up_weight)


def solution(mesh):
    placed = (P(("groups", "gx"), "gy"), P("gx", "gy"))
    return jax.shard_map(
        functools.partial(on_device, mesh.shape["gx"]),
        mesh=mesh,
        in_specs=placed,
        out_specs=P(("groups", "gy"), "gx"),
        check_vma=False,
    )
```

```python
import functools

import jax
import jax.numpy as jnp
from jax import lax
from jax.experimental import pallas as pl
from jax.experimental.pallas import tpu as pltpu
from jax.sharding import PartitionSpec as P

MESH = pl.DeviceIdType.MESH
SLACK = 0
LAG = 3


def ring_place(index, n):
    odd, half = lax.rem(index, 2), lax.div(index, 2)
    return odd * (n - 1 - half) + (1 - odd) * half


def ring_index(place, n):
    down = lax.div(place, n // 2)
    return (1 - down) * 2 * place + down * (2 * (n - 1 - place) + 1)


def kernel(
    n, pieces, halves, tiles, slots,
    tokens_ref, weight_ref, out_ref,
    gathered, weights, acc, parts, arrived, result,
    own_sem, weight_sem, send_sem, recv_sem, part_send, part_recv, out_sem,
):
    me, core = lax.axis_index("gx"), lax.axis_index("gy")
    rows, width = tokens_ref.shape[0], gathered.shape[2]
    block, tile = weights.shape[1], weights.shape[1] // tiles
    hops = n // 2
    place = ring_place(me, n)
    neighbours = tuple(ring_index(lax.rem(place + d, n), n) for d in (1, n - 1))
    blocks = pieces * halves

    def weight_copy(piece, half):
        slot = lax.rem(piece * halves + half, slots)
        return pltpu.make_async_copy(
            weight_ref.at[
                pl.ds(half * block, block), pl.ds(pl.multiple_of(piece * width, 128), width)
            ],
            weights.at[slot],
            weight_sem.at[slot],
        )

    def own_columns(piece):
        return tokens_ref.at[:, pl.ds(pl.multiple_of(piece * width, 128), width)]

    def rows_of(owner):
        return pl.ds(pl.multiple_of(owner * rows, rows), rows)

    def own_copy(piece):
        return pltpu.make_async_copy(
            own_columns(piece), gathered.at[piece, rows_of(me)], own_sem.at[piece]
        )

    def ring_copy(way, piece, hop):
        back = n - hop if way == 0 else hop
        held = gathered.at[piece, rows_of(ring_index(lax.rem(place + back, n), n))]
        return pltpu.make_async_remote_copy(
            src_ref=own_columns(piece) if hop == 0 else held,
            dst_ref=held,
            send_sem=send_sem.at[way, piece, hop],
            recv_sem=recv_sem.at[way, piece, hop],
            device_id={"gx": neighbours[way]},
            device_id_type=MESH,
        )

    def each_way(piece, hop, act):
        if hop < hops - 1:
            act(0)
            act(1)
        elif isinstance(piece, int):
            act(piece % 2)
        else:
            pl.when(lax.rem(piece, 2) == 0)(lambda: act(0))
            pl.when(lax.rem(piece, 2) == 1)(lambda: act(1))

    def stage(piece, hop):
        if hop >= 1:
            each_way(piece, hop - 1, lambda way: ring_copy(way, piece, hop - 1).wait_recv())
        if hop < hops:
            each_way(piece, hop, lambda way: ring_copy(way, piece, hop).start())

    def tick(step, extra):
        for hop in range(hops, -1, -1):
            if (extra - hop * LAG) % halves:
                continue
            piece = step + (extra - hop * LAG) // halves
            if isinstance(step, int):
                if 0 <= piece < pieces:
                    stage(piece, hop)
            else:
                pl.when(piece < pieces)(functools.partial(stage, piece, hop))

    for b in range(min(slots, blocks)):
        weight_copy(b // halves, b % halves).start()

    barrier = pltpu.get_barrier_semaphore()
    for neighbour in neighbours:
        pl.semaphore_signal(barrier, inc=1, device_id={"gx": neighbour}, device_id_type=MESH)
    pl.semaphore_signal(barrier, inc=1, device_id={"gy": 1 - core}, device_id_type=MESH)
    pl.semaphore_wait(barrier, 3)

    ahead = hops * LAG + SLACK
    tick(0, 0)
    for piece in range(pieces):
        own_copy(piece).start()
    for t in range(1, ahead):
        tick(t // halves, t % halves)
    acc[...] = jnp.zeros_like(acc)

    def product(piece, half, tile_at):
        slot = lax.rem(piece * halves + half, slots)
        at = pl.ds(tile_at[0], tile_at[1])
        return lax.dot_general(
            weights[slot, at, :], gathered[piece], (((1,), (1,)), ((), ())),
            preferred_element_type=jnp.float32,
        )

    @pl.loop(0, pieces - 1)
    def _(piece):
        for half in range(halves):
            tick(piece, half + ahead)
            if half == 0:
                own_copy(piece).wait()
            weight_copy(piece, half).wait()
            acc[pl.ds(half * block, block), :] += product(piece, half, (0, block))
            later = piece * halves + half + slots

            @pl.when(later < blocks)
            def _():
                weight_copy(lax.div(later, halves), lax.rem(later, halves)).start()

    last = pieces - 1
    for extra in range(halves):
        tick(last, extra + ahead)
    own_copy(last).wait()
    mine = parts.shape[1]

    def part_copy(j):
        at = pl.ds(j * tile, tile)
        return pltpu.make_async_remote_copy(
            src_ref=parts.at[1 - core, :, at],
            dst_ref=arrived.at[:, at],
            send_sem=part_send.at[j],
            recv_sem=part_recv.at[j],
            device_id={"gy": 1 - core},
            device_id_type=MESH,
        )

    def out_copy(j):
        at = pl.ds(j * tile, tile)
        return pltpu.make_async_copy(result.at[:, at], out_ref.at[:, at], out_sem.at[j])

    def combine(j):
        at = pl.ds(j * tile, tile)
        part_copy(j).wait_recv()
        result[:, at] = (parts[core, :, at] + arrived[:, at]).astype(result.dtype)
        out_copy(j).start()

    total = halves * tiles
    for j in range(total):
        half, within = j // tiles, j % tiles
        if within == 0:
            weight_copy(last, half).wait()
        summed = acc[pl.ds(j * tile, tile), :] + product(last, half, (within * tile, tile))
        turned = summed.T
        at = pl.ds(j * tile, tile)
        parts[0, :, at] = turned[:mine]
        parts[1, :, at] = turned[mine:]
        part_copy(j).start()
        if j >= 2:
            combine(j - 2)
    for j in range(max(total - 2, 0), total):
        combine(j)

    @pl.loop(0, pieces)
    def _(piece):
        for hop in range(hops):
            each_way(piece, hop, lambda way: ring_copy(way, piece, hop).wait_send())

    for j in range(total):
        part_copy(j).wait_send()
        out_copy(j).wait()


def on_device(n, tokens, up_weight):
    rows, depth = tokens.shape
    hidden = up_weight.shape[0]
    width = 1024 if depth % 1024 == 0 else 128
    pieces = depth // width
    halves = 2 if hidden % 256 == 0 else 1
    block = hidden // halves
    tiles = 2 if block % 256 == 0 else 1
    slots = min(8, pieces * halves)
    every, mine = rows * n, rows * n // 2
    dma = pltpu.SemaphoreType.DMA
    return pl.pallas_call(
        functools.partial(kernel, n, pieces, halves, tiles, slots),
        out_shape=jax.ShapeDtypeStruct((mine, hidden), jnp.bfloat16),
        in_specs=[pl.BlockSpec(memory_space=pl.ANY)] * 2,
        out_specs=pl.BlockSpec(memory_space=pl.ANY),
        scratch_shapes=[
            pltpu.VMEM((pieces, every, width), jnp.bfloat16),
            pltpu.VMEM((slots, block, width), jnp.bfloat16),
            pltpu.VMEM((hidden, every), jnp.float32),
            pltpu.VMEM((2, mine, hidden), jnp.float32),
            pltpu.VMEM((mine, hidden), jnp.float32),
            pltpu.VMEM((mine, hidden), jnp.bfloat16),
            dma((pieces,)),
            dma((slots,)),
            dma((2, pieces, n // 2)),
            dma((2, pieces, n // 2)),
            dma((halves * tiles,)),
            dma((halves * tiles,)),
            dma((halves * tiles,)),
        ],
        compiler_params=pltpu.CompilerParams(
            collective_id=0, has_side_effects=True, vmem_limit_bytes=58 * 2**20
        ),
        cost_estimate=pl.CostEstimate(
            flops=2 * every * hidden * depth, bytes_accessed=2 * hidden * depth, transcendentals=0
        ),
    )(tokens, up_weight)


def solution(mesh):
    placed = (P(("groups", "gx"), "gy"), P("gx", "gy"))
    return jax.shard_map(
        functools.partial(on_device, mesh.shape["gx"]),
        mesh=mesh,
        in_specs=placed,
        out_specs=P(("groups", "gy"), "gx"),
        check_vma=False,
    )
```
